32 devices in a mesh: grp: 4 (over y, core), dev: 8 (over z, x).
Axes of the slice: x: 2, y: 2, z: 4, core: 2. Of those that a mesh axis runs over, the one named last changes fastest.
Arguments:
- item_factors: bfloat16 [8192, 256], P(('grp', 'dev'))
- send_list: int32 [32, 4, 1], P(('grp', 'dev')), may hold values from 0 to 1
- route_list: int32 [32, 8, 1], P(('grp', 'dev')), may hold values from 0 to 3
- tile_slot: int32 [32, 64], P(('grp', 'dev')), may hold values from 0 to 7
- confidence: bfloat16 [2048, 128, 128], P(('grp', 'dev')), may hold values from 0 to 160, as said below
Outputs:
- user_factors: float32 [16384, 256], P(('grp', 'dev'))
The draws below stay inside these ranges and needn't reach their ends.
Inputs may be any that keep to these rules, and one draw needn't show every extreme that they name: `confidence`: every user row of every tile has at least one observed item.
All inputs are finite; a program needn't handle non-finite values.
Results may differ from the reference program's by a relative error of at most 0.0055.
Values may be sent and summed in bfloat16 or wider, within the bound.
No kernel may reach another device: no remote copies, remote signals or barrier semaphores. Data moves between devices by JAX's collectives and lax.ppermute only.
A program may use at most 128 MiB of HBM per device.

```python
import math
import jax
import jax.numpy as jnp
from jax import lax

RANK = 256
BLOCK = 128
PANELS_DEV = 2
SENT = 1
PICKED = 1
USER_BLOCKS = 4
TILES_PER = 16
ITERS = 8
TILES = 64
ALL_TILES = 2048
USERS = 16384
ITEMS = 8192
N_GRP = 4
N_DEV = 8


def draw_item_factors(key, part):
    key_base = jax.random.fold_in(jax.random.fold_in(key, 11), 0)
    key_column = jax.random.fold_in(jax.random.fold_in(key, 11), 3)
    position = jnp.arange(ITEMS, dtype=jnp.float32) / ITEMS
    row_scale = (1.0 + 2.0 * position) / math.sqrt(RANK)
    column_scale = jnp.exp(jax.random.uniform(key_column, (1, RANK), jnp.float32, math.log(0.3), 0.0))
    values = jax.random.normal(key_base, (ITEMS, RANK), jnp.float32)
    return (row_scale[:, None] * values * column_scale).astype(jnp.bfloat16)


def draw_confidence(key, part):
    key_mask, key_forced, key_value = jax.random.split(jax.random.fold_in(key, 23), 3)
    shape = (ALL_TILES, BLOCK, BLOCK)
    chance = jax.random.uniform(key_mask, shape, jnp.float32)
    forced = jax.random.randint(key_forced, (ALL_TILES, BLOCK, 1), 0, BLOCK)
    columns = jnp.arange(BLOCK, dtype=jnp.int32)[None, None, :]
    observed = jnp.logical_or(chance < 0.5, columns == forced)
    values = jnp.exp(jax.random.uniform(key_value, shape, jnp.float32, math.log(4.0), math.log(160.0)))
    return jnp.where(observed, values, 0.0).astype(jnp.bfloat16)


def set_ends(array, stream_key, smallest, high):
    longest = array.shape.index(max(array.shape))
    spots = []
    for shift in (0, 1):
        where = [jax.random.randint(jax.random.fold_in(stream_key, axis), (), 0, length) for axis, length in enumerate(array.shape)]
        where[longest] = (where[longest] + shift) % array.shape[longest]
        spots.append(tuple(where))
    return array.at[spots[0]].set(smallest).at[spots[1]].set(high)


def setup_inputs(seed: int = 0) -> dict:
    key_list = jax.random.split(jax.random.key(seed), 6)
    return {
        "item_factors": draw_item_factors(jax.random.fold_in(key_list[5], 71), 0),
        "send_list": set_ends(jax.random.randint(key_list[1], (N_GRP * N_DEV, N_GRP, SENT), 0, PANELS_DEV), jax.random.fold_in(key_list[1], 1), 0, PANELS_DEV - 1).astype(jnp.int32),
        "route_list": set_ends(jax.random.randint(key_list[2], (N_GRP * N_DEV, N_DEV, PICKED), 0, N_GRP * SENT), jax.random.fold_in(key_list[2], 1), 0, (N_GRP * SENT) - 1).astype(jnp.int32),
        "tile_slot": set_ends(jax.random.randint(key_list[3], (N_GRP * N_DEV, TILES), 0, N_DEV * PICKED), jax.random.fold_in(key_list[3], 1), 0, (N_DEV * PICKED) - 1).astype(jnp.int32),
        "confidence": draw_confidence(jax.random.fold_in(key_list[5], 71), 0),
    }


ridge = 0.1


def apply_operator(direction, gram, tile_panels, weights):
    dir_bf = direction.astype(jnp.bfloat16).astype(jnp.float32).reshape(USER_BLOCKS, BLOCK, RANK)
    panels32 = tile_panels.astype(jnp.float32)
    scores = jnp.einsum('ubr,utir->utbi', dir_bf, panels32)
    weighted = (weights.astype(jnp.float32) * scores).astype(jnp.bfloat16).astype(jnp.float32)
    back = jnp.einsum('utbi,utir->ubr', weighted, panels32).reshape(USER_BLOCKS * BLOCK, RANK)
    return jnp.dot(direction, gram, precision=lax.Precision.HIGHEST) + ridge * direction + back


def solve_users(gram, tile_panels, weights):
    observed = (weights > 0).astype(jnp.float32)
    target = ((1.0 + weights.astype(jnp.float32)) * observed).astype(jnp.bfloat16).astype(jnp.float32)
    right_side = jnp.einsum('utbi,utir->ubr', target, tile_panels.astype(jnp.float32)).reshape(USER_BLOCKS * BLOCK, RANK)
    solution = jnp.zeros_like(right_side)
    residual = right_side
    direction = right_side
    norm_now = jnp.sum(residual * residual, axis=1, keepdims=True)
    for step in range(ITERS):
        image = apply_operator(direction, gram, tile_panels, weights)
        alpha = norm_now / jnp.sum(direction * image, axis=1, keepdims=True)
        solution = solution + alpha * direction
        residual = residual - alpha * image
        norm_next = jnp.sum(residual * residual, axis=1, keepdims=True)
        direction = residual + (norm_next / norm_now) * direction
        norm_now = norm_next
    return solution


def reference(item_factors, send_list, route_list, tile_slot, confidence):
    devices = N_GRP * N_DEV
    gram = jnp.dot(item_factors.T, item_factors, preferred_element_type=jnp.float32)
    panels = item_factors.reshape(devices * PANELS_DEV, BLOCK, RANK)
    device_ids = jnp.arange(devices, dtype=jnp.int32)
    group_of = (device_ids // N_DEV)[:, None]
    member_of = (device_ids % N_DEV)[:, None]
    source_dev = (tile_slot // PICKED).astype(jnp.int32)
    picked_at = (tile_slot % PICKED).astype(jnp.int32)
    pool_index = route_list[group_of * N_DEV + source_dev, member_of, picked_at]
    anchor_group = (pool_index // SENT).astype(jnp.int32)
    sent_at = (pool_index % SENT).astype(jnp.int32)
    owner = anchor_group * N_DEV + source_dev
    local_panel = send_list[owner, group_of, sent_at]
    global_panel = (owner * PANELS_DEV + local_panel).astype(jnp.int32)
    weights_all = confidence.reshape(devices, USER_BLOCKS, TILES_PER, BLOCK, BLOCK)

    def one_device(pair):
        panel_ids, weights = pair
        tile_panels = panels[panel_ids].reshape(USER_BLOCKS, TILES_PER, BLOCK, RANK)
        return solve_users(gram, tile_panels, weights)

    solved = lax.map(one_device, (global_panel, weights_all))
    return solved.reshape(USERS, RANK)
```

```python
import functools

import jax
import jax.numpy as jnp
from jax import lax
from jax.experimental import pallas as pl
from jax.experimental.pallas import tpu as pltpu
from jax.sharding import PartitionSpec as P

RANK = 256
BLOCK = 128
PANELS_DEV = 2
USER_BLOCKS = 4
TILES_PER = 16
ITERS = 8
BF16 = jnp.bfloat16
F32 = jnp.float32

ridge = 0.1

VM = pl.BlockSpec(memory_space=pltpu.VMEM)
SM = pl.BlockSpec(memory_space=pltpu.SMEM)
params = pltpu.CompilerParams(vmem_limit_bytes=40 * 2**20)


def shape(rows, dtype=BF16):
    return jax.ShapeDtypeStruct((rows, RANK), dtype)


def call(body, name, in_specs, out_specs, out_shape, scratch=()):
    return pl.pallas_call(
        body,
        in_specs=in_specs,
        out_specs=out_specs,
        out_shape=out_shape,
        scratch_shapes=list(scratch),
        compiler_params=params,
        name=name,
    )


def own_panel(items, index):
    return items[pl.ds(pl.multiple_of(index * BLOCK, BLOCK), BLOCK), :]


def pack_core(send, items, out, gram_own, gram):
    group = lax.axis_index("grp")
    core = lax.rem(group, 2)
    out[0:BLOCK, :] = own_panel(items, send[0, group ^ 1, 0])
    out[BLOCK : 2 * BLOCK, :] = own_panel(items, send[0, group ^ 3, 0])
    rows = items[...]
    gram[...] = lax.dot_general(rows, rows, (((0,), (0,)), ((), ())), preferred_element_type=F32)
    out[2 * BLOCK : 3 * BLOCK, :] = own_panel(gram, 1 - core).astype(BF16)
    gram_own[...] = own_panel(gram, core)


def pack_y(send, items, gram_own, from_core, out, gram_sum):
    group = lax.axis_index("grp")
    out[0:BLOCK, :] = own_panel(items, send[0, group ^ 2, 0])
    out[BLOCK : 2 * BLOCK, :] = from_core[BLOCK : 2 * BLOCK, :]
    total = gram_own[...] + from_core[2 * BLOCK : 3 * BLOCK, :].astype(F32)
    out[2 * BLOCK : 3 * BLOCK, :] = total.astype(BF16)
    gram_sum[...] = total


def pack_dev(send, route, items, gram_own, from_core, from_y, *refs):
    outs, gram_sum, pool = refs[:8], refs[8], refs[9]
    group = lax.axis_index("grp")
    member = lax.axis_index("dev")
    pool[group] = own_panel(items, send[0, group, 0])
    pool[group ^ 1] = from_core[0:BLOCK, :]
    pool[group ^ 2] = from_y[0:BLOCK, :]
    pool[group ^ 3] = from_y[BLOCK : 2 * BLOCK, :]
    for step in range(8):
        outs[step][0:BLOCK, :] = pool[route[0, member ^ step, 0]]
    total = gram_own[...] + from_y[2 * BLOCK : 3 * BLOCK, :].astype(F32)
    outs[4][BLOCK : 2 * BLOCK, :] = total.astype(BF16)
    gram_sum[...] = total


def add_gram(gram_own, arrived, panel, out, gram_sum):
    total = gram_own[...] + arrived[BLOCK : 2 * BLOCK, :].astype(F32)
    out[0:BLOCK, :] = panel[...]
    out[BLOCK : 2 * BLOCK, :] = total.astype(BF16)
    gram_sum[...] = total


def last_gram(tile_slot, gram_own, arrived, out, gram_sum, places):
    total = gram_own[...] + arrived[BLOCK : 2 * BLOCK, :].astype(F32)
    out[...] = total.astype(BF16)
    gram_sum[...] = total
    member = lax.axis_index("dev")

    def place(tile, _):
        places[tile] = tile_slot[0, tile] ^ member
        return _

    lax.fori_loop(0, places.shape[0], place, 0)


def build_kernel(places, tiles, weights, high, low, target_sum):
    block = pl.program_id(0)
    weights[...] = jnp.zeros_like(weights)
    target_sum[...] = jnp.zeros_like(target_sum)
    for tile in range(TILES_PER):
        first = places[block * TILES_PER + tile] * BLOCK
        columns = pl.ds(pl.multiple_of(first, BLOCK), BLOCK)
        confidence = tiles[tile].astype(F32)
        target = jnp.where(confidence > 0, 1.0 + confidence, 0.0).astype(BF16)
        weights[:, columns] += confidence
        target_sum[:, columns] += target.astype(F32)
    total = target_sum[...]
    top = total.astype(BF16)
    high[...] = top
    low[...] = (total - top.astype(F32)).astype(BF16)


def build_weights(places, confidence, width):
    users = USER_BLOCKS * BLOCK
    return pl.pallas_call(
        build_kernel,
        grid_spec=pltpu.PrefetchScalarGridSpec(
            num_scalar_prefetch=1,
            grid=(USER_BLOCKS,),
            in_specs=[pl.BlockSpec((TILES_PER, BLOCK, BLOCK), lambda b, _: (b, 0, 0))],
            out_specs=[pl.BlockSpec((BLOCK, width), lambda b, _: (b, 0))] * 3,
            scratch_shapes=[pltpu.VMEM((BLOCK, width), F32)],
        ),
        out_shape=[
            jax.ShapeDtypeStruct((users, width), F32),
            jax.ShapeDtypeStruct((users, width), BF16),
            jax.ShapeDtypeStruct((users, width), BF16),
        ],
        compiler_params=params,
        name="build_weights",
    )(places, confidence)


def solve_kernel(count, chunk, halves, weights, high, low, *refs):
    gram_parts, panels = refs[:halves], refs[halves : halves + count]
    result, items, items_t, gram, residual_ref, direction_ref = refs[halves + count :]
    dot = functools.partial(jnp.dot, preferred_element_type=F32)
    for i in range(count):
        rows = slice(i * BLOCK, (i + 1) * BLOCK)
        panel = panels[i][0:BLOCK, :]
        items[rows, :] = panel
        items_t[:, rows] = panel.T
    if halves == 1:
        whole = gram_parts[0][...]
        top = whole.astype(BF16)
        gram[0] = top
        gram[1] = (whole - top.astype(F32)).astype(BF16)
    else:
        core = lax.rem(lax.axis_index("grp"), 2)
        mine = pl.ds(pl.multiple_of(core * BLOCK, BLOCK), BLOCK)
        other = pl.ds(pl.multiple_of((1 - core) * BLOCK, BLOCK), BLOCK)
        whole = gram_parts[0][...]
        top = whole.astype(BF16)
        gram[0, mine, :] = top
        gram[1, mine, :] = (whole - top.astype(F32)).astype(BF16)
        gram[0, other, :] = gram_parts[1][...]
        gram[1, other, :] = jnp.zeros((BLOCK, RANK), BF16)
    parts = [slice(i, i + chunk) for i in range(0, weights.shape[0], chunk)]
    norms = []
    for users in parts:
        right_side = dot(high[users, :], items[...]) + dot(low[users, :], items[...])
        residual_ref[users, :] = right_side
        direction_ref[users, :] = right_side
        result[users, :] = jnp.zeros_like(right_side)
        norms.append(jnp.sum(right_side * right_side, axis=1, keepdims=True))

    def step(_, norms):
        after = []
        for users, norm_now in zip(parts, norms):
            direction = direction_ref[users, :]
            top = direction.astype(BF16)
            rest = (direction - top.astype(F32)).astype(BF16)
            scores = dot(top, items_t[...])
            weighted = (weights[users, :] * scores).astype(BF16)
            image = dot(weighted, items[...])
            image = image + (dot(top, gram[0]) + (dot(rest, gram[0]) + dot(top, gram[1])))
            image = image + ridge * direction
            alpha = norm_now / jnp.sum(direction * image, axis=1, keepdims=True)
            result[users, :] += alpha * direction
            residual = residual_ref[users, :] - alpha * image
            residual_ref[users, :] = residual
            norm_next = jnp.sum(residual * residual, axis=1, keepdims=True)
            direction_ref[users, :] = residual + (norm_next / norm_now) * direction
            after.append(norm_next)
        return tuple(after)

    lax.fori_loop(0, ITERS, step, tuple(norms))


def solve_users(weights, high, low, gram_parts, panels, chunk=256):
    users, width = weights.shape
    return call(
        functools.partial(solve_kernel, len(panels), chunk, len(gram_parts)),
        "solve_users",
        [VM] * (3 + len(gram_parts) + len(panels)),
        VM,
        shape(users, F32),
        [
            pltpu.VMEM((width, RANK), BF16),
            pltpu.VMEM((RANK, width), BF16),
            pltpu.VMEM((2, RANK, RANK), BF16),
            pltpu.VMEM((users, RANK), F32),
            pltpu.VMEM((users, RANK), F32),
        ],
    )(weights, high, low, *gram_parts, *panels)


def swap(array, group_bits, member_bits):
    order = [
        (g * 8 + d, (g ^ group_bits) * 8 + (d ^ member_bits)) for g in range(4) for d in range(8)
    ]
    return lax.ppermute(array, ("grp", "dev"), order)


def shards_4x8(item_factors, send_list, route_list, tile_slot, confidence):
    tiles = tile_slot.shape[1]
    out, gram = call(
        pack_core, "pack_core", [SM, VM], [VM, VM],
        [shape(3 * BLOCK), shape(BLOCK, F32)], [pltpu.VMEM((RANK, RANK), F32)],
    )(send_list, item_factors)
    from_core = swap(out, 1, 0)
    out, gram = call(
        pack_y, "pack_y", [SM, VM, VM, VM], [VM, VM], [shape(3 * BLOCK), shape(BLOCK, F32)]
    )(send_list, item_factors, gram, from_core)
    from_y = swap(out, 2, 0)
    *outs, gram = call(
        pack_dev, "pack_dev", [SM, SM, VM, VM, VM, VM], [VM] * 9,
        [shape(2 * BLOCK if k == 4 else BLOCK) for k in range(8)] + [shape(BLOCK, F32)],
        [pltpu.VMEM((4, BLOCK, RANK), BF16)],
    )(send_list, route_list, item_factors, gram, from_core, from_y)
    panels = [outs[0]] + [None] * 7
    for k in (4, 5, 7, 6):
        panels[k] = swap(outs[k], 0, k)
    add = call(add_gram, "add_gram", [VM] * 3, [VM] * 2, [shape(2 * BLOCK), shape(BLOCK, F32)])
    out, gram = add(gram, panels[4], outs[1])
    panels[1] = swap(out, 0, 1)
    panels[3] = swap(outs[3], 0, 3)
    out, gram = add(gram, panels[1], outs[2])
    panels[2] = swap(out, 0, 2)
    out, gram, places = call(
        last_gram, "last_gram", [SM, VM, VM], [VM, VM, SM],
        [shape(BLOCK), shape(BLOCK, F32), jax.ShapeDtypeStruct((tiles,), jnp.int32)],
    )(tile_slot, gram, panels[2])
    other = swap(out, 1, 0)
    weights, high, low = build_weights(places, confidence, 8 * BLOCK)
    return solve_users(weights, high, low, [gram, other], panels)


def shards(item_factors, send_list, route_list, tile_slot, confidence):
    partial_gram = lax.dot_general(
        item_factors, item_factors, (((0,), (0,)), ((), ())), preferred_element_type=F32
    )
    gram = lax.psum(partial_gram, ("grp", "dev"))
    own_panels = item_factors.reshape(PANELS_DEV, BLOCK, RANK)
    outgoing = own_panels[send_list[0].reshape(-1)]
    group_pool = lax.all_to_all(outgoing, "grp", split_axis=0, concat_axis=0, tiled=True)
    picked = group_pool[route_list[0].reshape(-1)]
    arrived = lax.all_to_all(picked, "dev", split_axis=0, concat_axis=0, tiled=True)
    count = arrived.shape[0]
    weights, high, low = build_weights(tile_slot[0], confidence, count * BLOCK)
    return solve_users(weights, high, low, [gram], [arrived[i] for i in range(count)], BLOCK)


def solution(mesh):
    placed = (
        P(("grp", "dev"), None),
        P(("grp", "dev"), None, None),
        P(("grp", "dev"), None, None),
        P(("grp", "dev"), None),
        P(("grp", "dev"), None, None),
    )
    body = shards_4x8 if (mesh.shape["grp"], mesh.shape["dev"]) == (4, 8) else shards
    return jax.shard_map(
        body, mesh=mesh, in_specs=placed, out_specs=P(("grp", "dev"), None), check_vma=False
    )
```

```python
import functools

import jax
import jax.numpy as jnp
from jax import lax
from jax.experimental import pallas as pl
from jax.experimental.pallas import tpu as pltpu
from jax.sharding import PartitionSpec as P

RANK = 256
BLOCK = 128
PANELS_DEV = 2
USER_BLOCKS = 4
TILES_PER = 16
ITERS = 8
BF16 = jnp.bfloat16
F32 = jnp.float32

ridge = 0.1
COST = 1000000000
LEAD = 3000000000

VM = pl.BlockSpec(memory_space=pltpu.VMEM)
ANY = pl.BlockSpec(memory_space=pl.ANY)
SM = pl.BlockSpec(memory_space=pltpu.SMEM)


def params():
    return pltpu.CompilerParams(vmem_limit_bytes=40 * 2**20)


def shape(rows, dtype=BF16):
    return jax.ShapeDtypeStruct((rows, RANK), dtype)


def call(body, name, in_specs, out_specs, out_shape, scratch=(), cost=0):
    return pl.pallas_call(
        body,
        in_specs=in_specs,
        out_specs=out_specs,
        out_shape=out_shape,
        scratch_shapes=list(scratch),
        compiler_params=params(),
        cost_estimate=pl.CostEstimate(flops=cost, transcendentals=0, bytes_accessed=0),
        name=name,
    )


def own_panel(items, index):
    return items[pl.ds(pl.multiple_of(index * BLOCK, BLOCK), BLOCK), :]


def first_kernel(send_hbm, route_hbm, items_hbm, _, out, panel_y, panel_own, gram_own, picks, *scratch):
    send, route, items, gram, sems = scratch
    sources = (items_hbm, send_hbm, route_hbm)
    copies = [
        pltpu.make_async_copy(source, target, sems.at[i])
        for i, (source, target) in enumerate(zip(sources, (items, send, route)))
    ]
    for copy in copies:
        copy.start()
    group = lax.axis_index("grp")
    member = lax.axis_index("dev")
    core = lax.rem(group, 2)
    copies[0].wait()
    rows = items[...]
    gram[...] = lax.dot_general(rows, rows, (((0,), (0,)), ((), ())), preferred_element_type=F32)
    copies[1].wait()
    out[0:BLOCK, :] = own_panel(items, send[0, group ^ 1])
    out[BLOCK : 2 * BLOCK, :] = own_panel(items, send[0, group ^ 3])
    panel_y[...] = own_panel(items, send[0, group ^ 2])
    panel_own[...] = own_panel(items, send[0, group])
    out[2 * BLOCK : 3 * BLOCK, :] = own_panel(gram, 1 - core).astype(BF16)
    gram_own[...] = own_panel(gram, core)
    copies[2].wait()
    for step in range(8):
        picks[step : step + 1, :] = jnp.full((1, BLOCK), route[0, member ^ step] ^ group, jnp.int32)


def pack_y(panel_y, gram_own, from_core, out, gram_out, gram_sum):
    out[0:BLOCK, :] = panel_y[...]
    out[BLOCK : 2 * BLOCK, :] = from_core[BLOCK : 2 * BLOCK, :]
    total = gram_own[...] + from_core[2 * BLOCK : 3 * BLOCK, :].astype(F32)
    gram_out[...] = total.astype(BF16)
    gram_sum[...] = total


def pack_dev(picks, panel_own, from_core, from_y, *refs):
    outs, pool = refs[:8], refs[8]
    pool[0] = panel_own[...]
    pool[1] = from_core[0:BLOCK, :]
    pool[2] = from_y[0:BLOCK, :]
    pool[3] = from_y[BLOCK : 2 * BLOCK, :]
    for step in range(8):
        outs[step][...] = pool[jnp.max(picks[step : step + 1, :])]


def add_gram(gram_own, arrived, out, gram_sum):
    total = gram_own[...] + arrived[...].astype(F32)
    out[...] = total.astype(BF16)
    gram_sum[...] = total


def pack_near(gram_own, arrived, *refs):
    panels, outs, gram_sum = refs[:3], refs[4:7], refs[7]
    total = gram_own[...] + arrived[...].astype(F32)
    gram_sum[...] = total
    for panel, out in zip(panels, outs):
        out[0:BLOCK, :] = panel[...]
        out[BLOCK : 2 * BLOCK, :] = total.astype(BF16)


def last_gram(gram_own, *refs):
    out, gram_sum = refs[-2:]
    total = gram_own[...]
    for part in refs[:3]:
        total += part[BLOCK : 2 * BLOCK, :].astype(F32)
    out[...] = total.astype(BF16)
    gram_sum[...] = total


def touch(*refs):
    refs[-1][...] = jnp.zeros_like(refs[-1])


def after(cost, *arrays):
    return call(
        touch, "after", [ANY] * len(arrays), VM, jax.ShapeDtypeStruct((8, BLOCK), F32), cost=cost
    )(*arrays)


def build_kernel(mixed, slots, tiles, _, weights, high, low, target_sum):
    block = pl.program_id(0)
    turn = lax.axis_index("dev") if mixed else 0
    weights[...] = jnp.zeros_like(weights)
    target_sum[...] = jnp.zeros_like(target_sum)
    for tile in range(TILES_PER):
        first = (slots[0, block * TILES_PER + tile] ^ turn) * BLOCK
        columns = pl.ds(pl.multiple_of(first, BLOCK), BLOCK)
        confidence = tiles[tile].astype(F32)
        target = jnp.where(confidence > 0, 1.0 + confidence, 0.0).astype(BF16)
        weights[:, columns] += confidence
        target_sum[:, columns] += target.astype(F32)
    total = target_sum[...]
    top = total.astype(BF16)
    high[...] = top
    low[...] = (total - top.astype(F32)).astype(BF16)


def build_weights(slots, confidence, after, width, mixed):
    users = USER_BLOCKS * BLOCK
    return pl.pallas_call(
        functools.partial(build_kernel, mixed),
        grid_spec=pltpu.PrefetchScalarGridSpec(
            num_scalar_prefetch=1,
            grid=(USER_BLOCKS,),
            in_specs=[pl.BlockSpec((TILES_PER, BLOCK, BLOCK), lambda b, _: (b, 0, 0)), ANY],
            out_specs=[pl.BlockSpec((BLOCK, width), lambda b, _: (b, 0))] * 3,
            scratch_shapes=[pltpu.VMEM((BLOCK, width), F32)],
        ),
        out_shape=[
            jax.ShapeDtypeStruct((users, width), F32),
            jax.ShapeDtypeStruct((users, width), BF16),
            jax.ShapeDtypeStruct((users, width), BF16),
        ],
        compiler_params=params(),
        name="build_weights",
    )(slots, confidence, after)


def right_kernel(count, chunk, weights, high, low, *refs):
    panels, (items, items_t, right_side, image) = refs[:count], refs[count + 1 :]
    dot = functools.partial(jnp.dot, preferred_element_type=F32)
    for i in range(count):
        rows = slice(i * BLOCK, (i + 1) * BLOCK)
        panel = panels[i][0:BLOCK, :]
        items[rows, :] = panel
        items_t[:, rows] = panel.T
    for start in range(0, weights.shape[0], chunk):
        users = slice(start, start + chunk)
        target = dot(high[users, :], items[...]) + dot(low[users, :], items[...])
        right_side[users, :] = target
        scores = dot(target.astype(BF16), items_t[...])
        image[users, :] = dot((weights[users, :] * scores).astype(BF16), items[...])


def solve_kernel(halves, chunk, weights, items, items_t, right_side, first_image, *refs):
    gram_parts = refs[:halves]
    result, gram, residual_ref, direction_ref = refs[halves:]
    dot = functools.partial(jnp.dot, preferred_element_type=F32)
    whole = gram_parts[0][...]
    top = whole.astype(BF16)
    rest = (whole - top.astype(F32)).astype(BF16)
    if halves == 1:
        gram[0] = top
        gram[1] = rest
    else:
        core = lax.rem(lax.axis_index("grp"), 2)
        mine = pl.ds(pl.multiple_of(core * BLOCK, BLOCK), BLOCK)
        other = pl.ds(pl.multiple_of((1 - core) * BLOCK, BLOCK), BLOCK)
        gram[0, mine, :] = top
        gram[1, mine, :] = rest
        gram[0, other, :] = gram_parts[1][...]
        gram[1, other, :] = jnp.zeros((BLOCK, RANK), BF16)
    parts = [slice(i, i + chunk) for i in range(0, weights.shape[0], chunk)]

    def advance(users, norm_now, direction, residual, solved, image):
        top = direction.astype(BF16)
        rest = (direction - top.astype(F32)).astype(BF16)
        if image is None:
            scores = dot(top, items_t[...])
            image = dot((weights[users, :] * scores).astype(BF16), items[...])
        image = image + (dot(top, gram[0]) + (dot(rest, gram[0]) + dot(top, gram[1])))
        image = image + ridge * direction
        alpha = norm_now / jnp.sum(direction * image, axis=1, keepdims=True)
        moved = alpha * direction
        result[users, :] = moved if solved is None else solved + moved
        residual = residual - alpha * image
        residual_ref[users, :] = residual
        norm_next = jnp.sum(residual * residual, axis=1, keepdims=True)
        direction_ref[users, :] = residual + (norm_next / norm_now) * direction
        return norm_next

    norms = []
    for users in parts:
        start = right_side[users, :]
        norm = jnp.sum(start * start, axis=1, keepdims=True)
        norms.append(advance(users, norm, start, start, None, first_image[users, :]))

    def step(_, norms):
        return tuple(
            advance(users, norm, direction_ref[users, :], residual_ref[users, :], result[users, :], None)
            for users, norm in zip(parts, norms)
        )

    lax.fori_loop(1, ITERS, step, tuple(norms))


def start_solve(weights, high, low, panels, after, chunk=256):
    users, width = weights.shape
    return call(
        functools.partial(right_kernel, len(panels), chunk), "right_side",
        [VM] * (3 + len(panels)) + [ANY], [VM] * 4,
        [shape(width), jax.ShapeDtypeStruct((RANK, width), BF16), shape(users, F32), shape(users, F32)],
    )(weights, high, low, *panels, after)


def solve_users(weights, started, gram_parts, chunk=256):
    users = weights.shape[0]
    return call(
        functools.partial(solve_kernel, len(gram_parts), chunk), "solve_users",
        [VM] * (5 + len(gram_parts)), VM, shape(users, F32),
        [pltpu.VMEM((2, RANK, RANK), BF16), pltpu.VMEM((users, RANK), F32), pltpu.VMEM((users, RANK), F32)],
    )(weights, *started, *gram_parts)


def swap(array, group_bits, member_bits):
    order = [
        (g * 8 + d, (g ^ group_bits) * 8 + (d ^ member_bits)) for g in range(4) for d in range(8)
    ]
    return lax.ppermute(array, ("grp", "dev"), order)


def shards_4x8(item_factors, send_list, route_list, tile_slot, confidence):
    send_list, route_list = send_list.reshape(1, -1), route_list.reshape(1, -1)
    half, both = shape(BLOCK), shape(2 * BLOCK)
    total = shape(BLOCK, F32)
    out, panel_y, panel_own, gram, picks = call(
        first_kernel, "first", [ANY] * 4, [VM] * 5,
        [shape(3 * BLOCK), half, half, total, jax.ShapeDtypeStruct((8, BLOCK), jnp.int32)],
        [
            pltpu.SMEM(send_list.shape, jnp.int32), pltpu.SMEM(route_list.shape, jnp.int32),
            pltpu.VMEM(item_factors.shape, BF16), pltpu.VMEM((RANK, RANK), F32),
            pltpu.SemaphoreType.DMA((3,)),
        ],
    )(send_list, route_list, item_factors, after(LEAD))
    from_core = swap(out, 1, 0)
    out, gram_out, gram = call(pack_y, "pack_y", [VM] * 3, [VM] * 3, [both, half, total])(
        panel_y, gram, from_core
    )
    from_y = swap(out, 2, 0)
    gram_in = swap(gram_out, 0, 4)
    outs = call(
        pack_dev, "pack_dev", [VM] * 4, [VM] * 8, [half] * 8, [pltpu.VMEM((4, BLOCK, RANK), BF16)]
    )(picks, panel_own, from_core, from_y)
    panels = [outs[0]] + [None] * 7
    for k in (5, 4, 7, 6):
        panels[k] = swap(outs[k], 0, k)
    gram_out, gram = call(add_gram, "add_gram", [VM] * 2, [VM] * 2, [half, total])(gram, gram_in)
    gram_in = swap(gram_out, 2, 0)
    token = after(COST, panels[5])
    *near, gram = call(pack_near, "pack_near", [VM] * 5 + [ANY], [VM] * 4, [both] * 3 + [total])(
        gram, gram_in, outs[1], outs[2], outs[3], token
    )
    for k in (3, 2, 1):
        panels[k] = swap(near[k - 1], 0, k)
    weights, high, low = build_weights(tile_slot, confidence, after(0, panels[7], gram), 8 * BLOCK, True)
    token = after(COST, panels[7], panels[6])
    out, gram = call(last_gram, "last_gram", [VM] * 4 + [ANY] * 2, [VM] * 2, [half, total])(
        gram, panels[3], panels[2], panels[1], token, high
    )
    other = swap(out, 1, 0)
    started = start_solve(weights, high, low, panels, gram)
    return solve_users(weights, started, [gram, other])


def shards(item_factors, send_list, route_list, tile_slot, confidence):
    partial_gram = lax.dot_general(
        item_factors, item_factors, (((0,), (0,)), ((), ())), preferred_element_type=F32
    )
    gram = lax.psum(partial_gram, ("grp", "dev"))
    own_panels = item_factors.reshape(PANELS_DEV, BLOCK, RANK)
    outgoing = own_panels[send_list[0].reshape(-1)]
    group_pool = lax.all_to_all(outgoing, "grp", split_axis=0, concat_axis=0, tiled=True)
    picked = group_pool[route_list[0].reshape(-1)]
    arrived = lax.all_to_all(picked, "dev", split_axis=0, concat_axis=0, tiled=True)
    count = arrived.shape[0]
    weights, high, low = build_weights(tile_slot, confidence, gram, count * BLOCK, False)
    started = start_solve(weights, high, low, [arrived[i] for i in range(count)], gram, BLOCK)
    return solve_users(weights, started, [gram], BLOCK)


def solution(mesh):
    placed = (
        P(("grp", "dev"), None),
        P(("grp", "dev"), None, None),
        P(("grp", "dev"), None, None),
        P(("grp", "dev"), None),
        P(("grp", "dev"), None, None),
    )
    body = shards_4x8 if (mesh.shape["grp"], mesh.shape["dev"]) == (4, 8) else shards
    return jax.shard_map(
        body, mesh=mesh, in_specs=placed, out_specs=P(("grp", "dev"), None), check_vma=False
    )
```

```python
import functools

import jax
import jax.numpy as jnp
from jax import lax
from jax.experimental import pallas as pl
from jax.experimental.pallas import tpu as pltpu
from jax.sharding import PartitionSpec as P

RANK = 256
BLOCK = 128
PANELS_DEV = 2
USER_BLOCKS = 4
TILES_PER = 16
ITERS = 8
BF16 = jnp.bfloat16
F32 = jnp.float32

ridge = 0.1
COST = 1000000000
LEAD = 3000000000

VM = pl.BlockSpec(memory_space=pltpu.VMEM)
ANY = pl.BlockSpec(memory_space=pl.ANY)
SM = pl.BlockSpec(memory_space=pltpu.SMEM)


def params():
    return pltpu.CompilerParams(vmem_limit_bytes=40 * 2**20)


def shape(rows, dtype=BF16):
    return jax.ShapeDtypeStruct((rows, RANK), dtype)


def call(body, name, in_specs, out_specs, out_shape, scratch=(), cost=0):
    return pl.pallas_call(
        body,
        in_specs=in_specs,
        out_specs=out_specs,
        out_shape=out_shape,
        scratch_shapes=list(scratch),
        compiler_params=params(),
        cost_estimate=None if cost is None else pl.CostEstimate(flops=cost, transcendentals=0, bytes_accessed=0),
        name=name,
    )


def own_panel(items, index):
    return items[pl.ds(pl.multiple_of(index * BLOCK, BLOCK), BLOCK), :]


def entry(row, index):
    place = lax.broadcasted_iota(jnp.int32, row.shape, 1)
    return jnp.max(jnp.where(place == index, row, 0))


def first_kernel(send, route, items, _, out, panel_y, panel_own, gram_own, picks, gram):
    group = lax.axis_index("grp")
    member = lax.axis_index("dev")
    core = lax.rem(group, 2)
    panels, routes = send[...], route[...]
    out[0:BLOCK, :] = own_panel(items, entry(panels, group ^ 1))
    out[BLOCK : 2 * BLOCK, :] = own_panel(items, entry(panels, group ^ 3))
    panel_y[...] = own_panel(items, entry(panels, group ^ 2))
    panel_own[...] = own_panel(items, entry(panels, group))
    rows = items[...]
    gram[...] = lax.dot_general(rows, rows, (((0,), (0,)), ((), ())), preferred_element_type=F32)
    out[2 * BLOCK : 3 * BLOCK, :] = own_panel(gram, 1 - core).astype(BF16)
    gram_own[...] = own_panel(gram, core)
    for step in range(8):
        picks[step : step + 1, :] = jnp.full((1, BLOCK), entry(routes, member ^ step) ^ group, jnp.int32)


def pack_y(panel_y, gram_own, from_core, out, gram_out, gram_sum):
    out[0:BLOCK, :] = panel_y[...]
    out[BLOCK : 2 * BLOCK, :] = from_core[BLOCK : 2 * BLOCK, :]
    total = gram_own[...] + from_core[2 * BLOCK : 3 * BLOCK, :].astype(F32)
    gram_out[...] = total.astype(BF16)
    gram_sum[...] = total


def pack_dev(picks, panel_own, from_core, from_y, *refs):
    outs, pool = refs[:8], refs[8]
    pool[0] = panel_own[...]
    pool[1] = from_core[0:BLOCK, :]
    pool[2] = from_y[0:BLOCK, :]
    pool[3] = from_y[BLOCK : 2 * BLOCK, :]
    for step in range(8):
        outs[step][...] = pool[jnp.max(picks[step : step + 1, :])]


def add_gram(gram_own, arrived, out, gram_sum):
    total = gram_own[...] + arrived[...].astype(F32)
    out[...] = total.astype(BF16)
    gram_sum[...] = total


def pack_near(gram_own, arrived, *refs):
    panels, outs, gram_sum = refs[:3], refs[4:7], refs[7]
    total = gram_own[...] + arrived[...].astype(F32)
    gram_sum[...] = total
    for panel, out in zip(panels, outs):
        out[0:BLOCK, :] = panel[...]
        out[BLOCK : 2 * BLOCK, :] = total.astype(BF16)


def last_gram(gram_own, *refs):
    out, gram_sum = refs[-2:]
    total = gram_own[...]
    for part in refs[:3]:
        total += part[BLOCK : 2 * BLOCK, :].astype(F32)
    out[...] = total.astype(BF16)
    gram_sum[...] = total


def touch(*refs):
    refs[-1][...] = jnp.zeros_like(refs[-1])


def after(cost, *arrays):
    return call(
        touch, "after", [ANY] * len(arrays), VM, jax.ShapeDtypeStruct((8, BLOCK), F32), cost=cost
    )(*arrays)


def build_kernel(mixed, slots, tiles, _, *refs):
    weights, high, low, target_sum = (refs[i : i + USER_BLOCKS] for i in range(0, 4 * USER_BLOCKS, USER_BLOCKS))
    turn = lax.axis_index("dev") if mixed else 0
    for ref in weights + target_sum:
        ref[...] = jnp.zeros_like(ref)
    for tile in range(TILES_PER):
        for block in range(USER_BLOCKS):
            index = block * TILES_PER + tile
            first = (slots[0, index] ^ turn) * BLOCK
            columns = pl.ds(pl.multiple_of(first, BLOCK), BLOCK)
            confidence = tiles[index].astype(F32)
            target = jnp.where(confidence > 0, 1.0 + confidence, 0.0).astype(BF16)
            weights[block][:, columns] += confidence
            target_sum[block][:, columns] += target.astype(F32)
    for block in range(USER_BLOCKS):
        total = target_sum[block][...]
        top = total.astype(BF16)
        high[block][...] = top
        low[block][...] = (total - top.astype(F32)).astype(BF16)


def build_weights(slots, confidence, after, width, mixed):
    wide = jax.ShapeDtypeStruct((BLOCK, width), F32)
    narrow = jax.ShapeDtypeStruct((BLOCK, width), BF16)
    return call(
        functools.partial(build_kernel, mixed), "build_weights", [SM, VM, ANY],
        [VM] * 3 * USER_BLOCKS, [wide] * USER_BLOCKS + [narrow] * 2 * USER_BLOCKS,
        [pltpu.VMEM((BLOCK, width), F32)] * USER_BLOCKS, cost=None,
    )(slots, confidence, after)


def right_kernel(count, *refs):
    weights, high, low = (refs[i : i + USER_BLOCKS] for i in range(0, 3 * USER_BLOCKS, USER_BLOCKS))
    panels = refs[3 * USER_BLOCKS : 3 * USER_BLOCKS + count]
    items, items_t, right_side, image = refs[-4:]
    dot = functools.partial(jnp.dot, preferred_element_type=F32)
    for i in range(count):
        rows = slice(i * BLOCK, (i + 1) * BLOCK)
        panel = panels[i][0:BLOCK, :]
        items[rows, :] = panel
        items_t[:, rows] = panel.T
    for block in range(USER_BLOCKS):
        users = slice(block * BLOCK, (block + 1) * BLOCK)
        target = dot(high[block][...], items[...]) + dot(low[block][...], items[...])
        right_side[users, :] = target
        scores = dot(target.astype(BF16), items_t[...])
        image[users, :] = dot((weights[block][...] * scores).astype(BF16), items[...])


def start_solve(built, panels, after):
    width = built[0].shape[1]
    users = USER_BLOCKS * BLOCK
    return call(
        functools.partial(right_kernel, len(panels)), "right_side",
        [VM] * (len(built) + len(panels)) + [ANY], [VM] * 4,
        [shape(width), jax.ShapeDtypeStruct((RANK, width), BF16), shape(users, F32), shape(users, F32)],
        cost=None,
    )(*built, *panels, after)


def solve_kernel(halves, unroll, *refs):
    weights, refs = refs[:USER_BLOCKS], refs[USER_BLOCKS:]
    items, items_t, right_side, first_image = refs[:4]
    gram_parts, result, gram, sems = refs[4 : 4 + halves], refs[4 + halves], refs[5 + halves], refs[6 + halves]
    state = refs[7 + halves :]
    residuals, directions, solved = (state[i : i + USER_BLOCKS] for i in range(0, 3 * USER_BLOCKS, USER_BLOCKS))
    dot = functools.partial(jnp.dot, preferred_element_type=F32)
    if halves == 1:
        gram[...] = gram_parts[0][...].astype(BF16)
    else:
        core = lax.rem(lax.axis_index("grp"), 2)
        for place, part in zip((core, 1 - core), gram_parts):
            gram[pl.ds(pl.multiple_of(place * BLOCK, BLOCK), BLOCK), :] = part[...].astype(BF16)

    def rows(block):
        return slice(block * BLOCK, (block + 1) * BLOCK)

    def image_of(block, direction, scores):
        weighted = (weights[block][...] * scores).astype(BF16)
        return dot(weighted, items[...]) + dot(direction.astype(BF16), gram[...])

    def advance(block, norm_now, direction, residual, image, last=False):
        image = image + ridge * direction
        alpha = norm_now / jnp.sum(direction * image, axis=1, keepdims=True)
        solved[block][...] += alpha * direction
        if last:
            return norm_now
        residual = residual - alpha * image
        residuals[block][...] = residual
        norm_next = jnp.sum(residual * residual, axis=1, keepdims=True)
        directions[block][...] = residual + (norm_next / norm_now) * direction
        return norm_next

    norms = []
    for block in range(USER_BLOCKS):
        start = right_side[rows(block), :]
        solved[block][...] = jnp.zeros_like(start)
        norm = jnp.sum(start * start, axis=1, keepdims=True)
        image = first_image[rows(block), :] + dot(start.astype(BF16), gram[...])
        norms.append(advance(block, norm, start, start, image))

    copies = [
        pltpu.make_async_copy(solved[block], result.at[pl.ds(block * BLOCK, BLOCK), :], sems.at[block])
        for block in range(USER_BLOCKS)
    ]

    def step(_, norms, last=False):
        after = []
        for first in range(0, USER_BLOCKS, 2):
            pair = (first, first + 1)
            now = [directions[block][...] for block in pair]
            scores = [dot(direction.astype(BF16), items_t[...]) for direction in now]
            images = [image_of(*each) for each in zip(pair, now, scores)]
            for block, direction, image in zip(pair, now, images):
                after.append(advance(block, norms[block], direction, residuals[block][...], image, last))
                if last:
                    copies[block].start()
        return tuple(after)

    norms = lax.fori_loop(1, ITERS - 1, step, tuple(norms), unroll=unroll)
    step(None, norms, True)
    for copy in copies:
        copy.wait()


def solve_users(weights, started, gram_parts, unroll=True):
    users = USER_BLOCKS * BLOCK
    return call(
        functools.partial(solve_kernel, len(gram_parts), unroll), "solve_users",
        [VM] * (USER_BLOCKS + 4 + len(gram_parts)), ANY, shape(users, F32),
        [pltpu.VMEM((RANK, RANK), BF16), pltpu.SemaphoreType.DMA((USER_BLOCKS,))]
        + [pltpu.VMEM((BLOCK, RANK), F32)] * 3 * USER_BLOCKS,
        cost=None,
    )(*weights, *started, *gram_parts)


def swap(array, group_bits, member_bits):
    order = [
        (g * 8 + d, (g ^ group_bits) * 8 + (d ^ member_bits)) for g in range(4) for d in range(8)
    ]
    return lax.ppermute(array, ("grp", "dev"), order)


def shards_4x8(item_factors, send_list, route_list, tile_slot, confidence):
    send_list, route_list = send_list.reshape(1, -1), route_list.reshape(1, -1)
    half, both = shape(BLOCK), shape(2 * BLOCK)
    total = shape(BLOCK, F32)
    out, panel_y, panel_own, gram, picks = call(
        first_kernel, "first", [VM] * 3 + [ANY], [VM] * 5,
        [shape(3 * BLOCK), half, half, total, jax.ShapeDtypeStruct((8, BLOCK), jnp.int32)],
        [pltpu.VMEM((RANK, RANK), F32)],
    )(send_list, route_list, item_factors, after(LEAD))
    from_core = swap(out, 1, 0)
    out, gram_out, gram = call(pack_y, "pack_y", [VM] * 3, [VM] * 3, [both, half, total])(
        panel_y, gram, from_core
    )
    from_y = swap(out, 2, 0)
    gram_in = swap(gram_out, 0, 4)
    outs = call(
        pack_dev, "pack_dev", [VM] * 4, [VM] * 8, [half] * 8, [pltpu.VMEM((4, BLOCK, RANK), BF16)]
    )(picks, panel_own, from_core, from_y)
    panels = [outs[0]] + [None] * 7
    for k in (4, 6, 5, 7):
        panels[k] = swap(outs[k], 0, k)
    gram_out, gram = call(add_gram, "add_gram", [VM] * 2, [VM] * 2, [half, total])(gram, gram_in)
    gram_in = swap(gram_out, 2, 0)
    token = after(COST, panels[4])
    *near, gram = call(pack_near, "pack_near", [VM] * 5 + [ANY], [VM] * 4, [both] * 3 + [total])(
        gram, gram_in, outs[1], outs[2], outs[3], token
    )
    for k in (3, 2, 1):
        panels[k] = swap(near[k - 1], 0, k)
    built = build_weights(tile_slot, confidence, after(0, panels[6], gram), 8 * BLOCK, True)
    token = after(COST, panels[5], panels[7])
    out, gram = call(last_gram, "last_gram", [VM] * 4 + [ANY] * 2, [VM] * 2, [half, total])(
        gram, panels[3], panels[2], panels[1], token, built[-1]
    )
    other = swap(out, 1, 0)
    started = start_solve(built, panels, gram)
    return solve_users(built[:USER_BLOCKS], started, [gram, other])


def shards(item_factors, send_list, route_list, tile_slot, confidence):
    partial_gram = lax.dot_general(
        item_factors, item_factors, (((0,), (0,)), ((), ())), preferred_element_type=F32
    )
    gram = lax.psum(partial_gram, ("grp", "dev"))
    own_panels = item_factors.reshape(PANELS_DEV, BLOCK, RANK)
    outgoing = own_panels[send_list[0].reshape(-1)]
    group_pool = lax.all_to_all(outgoing, "grp", split_axis=0, concat_axis=0, tiled=True)
    picked = group_pool[route_list[0].reshape(-1)]
    arrived = lax.all_to_all(picked, "dev", split_axis=0, concat_axis=0, tiled=True)
    count = arrived.shape[0]
    built = build_weights(tile_slot, confidence, gram, count * BLOCK, False)
    started = start_solve(built, [arrived[i] for i in range(count)], gram)
    return solve_users(built[:USER_BLOCKS], started, [gram], 1)


def solution(mesh):
    placed = (
        P(("grp", "dev"), None),
        P(("grp", "dev"), None, None),
        P(("grp", "dev"), None, None),
        P(("grp", "dev"), None),
        P(("grp", "dev"), None, None),
    )
    body = shards_4x8 if (mesh.shape["grp"], mesh.shape["dev"]) == (4, 8) else shards
    return jax.shard_map(
        body, mesh=mesh, in_specs=placed, out_specs=P(("grp", "dev"), None), check_vma=False
    )
```

```python
import functools

import jax
import jax.numpy as jnp
from jax import lax
from jax.experimental import pallas as pl
from jax.experimental.pallas import tpu as pltpu
from jax.sharding import PartitionSpec as P

RANK = 256
BLOCK = 128
PANELS_DEV = 2
USER_BLOCKS = 4
TILES_PER = 16
ITERS = 8
BF16 = jnp.bfloat16
F32 = jnp.float32

HALF = BLOCK // 2
PART = 3 * HALF // 2

ridge = 0.1
COST = 1000000000
LEAD = 3000000000

VM = pl.BlockSpec(memory_space=pltpu.VMEM)
ANY = pl.BlockSpec(memory_space=pl.ANY)
SM = pl.BlockSpec(memory_space=pltpu.SMEM)


def params():
    return pltpu.CompilerParams(vmem_limit_bytes=40 * 2**20)


def shape(rows, dtype=BF16):
    return jax.ShapeDtypeStruct((rows, RANK), dtype)


def call(body, name, in_specs, out_specs, out_shape, scratch=(), cost=0):
    return pl.pallas_call(
        body,
        in_specs=in_specs,
        out_specs=out_specs,
        out_shape=out_shape,
        scratch_shapes=list(scratch),
        compiler_params=params(),
        cost_estimate=None if cost is None else pl.CostEstimate(flops=cost, transcendentals=0, bytes_accessed=0),
        name=name,
    )


def own_panel(items, index):
    return items[pl.ds(pl.multiple_of(index * BLOCK, BLOCK), BLOCK), :]


def entry(row, index):
    place = lax.broadcasted_iota(jnp.int32, row.shape, 1)
    return jnp.max(jnp.where(place == index, row, 0))


def pack_gram(gram, parts):
    for core in range(2):
        rows = slice(core * BLOCK, (core + 1) * BLOCK)
        square = gram[rows, rows]
        side = gram[core * HALF : (core + 1) * HALF, BLOCK:]
        parts[core, 0:HALF, 0:BLOCK] = square[0:HALF, :]
        parts[core, 0:HALF, BLOCK:] = square[HALF:, :]
        parts[core, HALF:, 0:BLOCK] = side[0 : HALF // 2, :]
        parts[core, HALF:, BLOCK:] = side[HALF // 2 :, :]


def unpack_gram(parts, gram):
    for core in range(2):
        rows = slice(core * BLOCK, (core + 1) * BLOCK)
        half = slice(core * HALF, (core + 1) * HALF)
        part = parts[core]
        gram[rows, rows] = jnp.concatenate([part[0:HALF, 0:BLOCK], part[0:HALF, BLOCK:]], axis=0).astype(BF16)
        side = jnp.concatenate([part[HALF:, 0:BLOCK], part[HALF:, BLOCK:]], axis=0)
        gram[half, BLOCK:] = side.astype(BF16)
    gram[BLOCK:, 0:BLOCK] = gram[0:BLOCK, BLOCK:].T


def first_kernel(send, route, items, _, out, panel_y, panel_own, gram_own, picks, gram, parts):
    group = lax.axis_index("grp")
    member = lax.axis_index("dev")
    core = lax.rem(group, 2)
    panels, routes = send[...], route[...]
    out[0:BLOCK, :] = own_panel(items, entry(panels, group ^ 1))
    out[BLOCK : 2 * BLOCK, :] = own_panel(items, entry(panels, group ^ 3))
    panel_y[...] = own_panel(items, entry(panels, group ^ 2))
    panel_own[...] = own_panel(items, entry(panels, group))
    rows = items[...]
    gram[...] = lax.dot_general(rows, rows, (((0,), (0,)), ((), ())), preferred_element_type=F32)
    pack_gram(gram, parts)
    out[2 * BLOCK :, :] = parts[1 - core].astype(BF16)
    gram_own[...] = parts[core]
    for step in range(8):
        picks[step : step + 1, :] = jnp.full((1, BLOCK), entry(routes, member ^ step) ^ group, jnp.int32)


def pack_y(panel_y, gram_own, from_core, out, gram_out, gram_sum):
    out[0:BLOCK, :] = panel_y[...]
    out[BLOCK : 2 * BLOCK, :] = from_core[BLOCK : 2 * BLOCK, :]
    total = gram_own[...] + from_core[2 * BLOCK :, :].astype(F32)
    gram_out[...] = total.astype(BF16)
    gram_sum[...] = total


def pack_dev(picks, panel_own, from_core, from_y, *refs):
    outs, pool = refs[:8], refs[8]
    pool[0] = panel_own[...]
    pool[1] = from_core[0:BLOCK, :]
    pool[2] = from_y[0:BLOCK, :]
    pool[3] = from_y[BLOCK : 2 * BLOCK, :]
    for step in range(8):
        outs[step][...] = pool[jnp.max(picks[step : step + 1, :])]


def add_gram(gram_own, arrived, _, out, gram_sum):
    total = gram_own[...] + arrived[...].astype(F32)
    out[...] = total.astype(BF16)
    gram_sum[...] = total


def pack_near(gram_own, arrived, *refs):
    panels, outs, gram_sum = refs[:3], refs[4:7], refs[7]
    total = gram_own[...] + arrived[...].astype(F32)
    gram_sum[...] = total
    for panel, out in zip(panels, outs):
        out[0:BLOCK, :] = panel[...]
        out[BLOCK:, :] = total.astype(BF16)


def last_gram(gram_own, *refs):
    out, gram_sum = refs[-2:]
    total = gram_own[...]
    for part in refs[:3]:
        total += part[BLOCK:, :].astype(F32)
    out[...] = total.astype(BF16)
    gram_sum[...] = total


def touch(*refs):
    refs[-1][...] = jnp.zeros_like(refs[-1])


def after(cost, *arrays):
    return call(
        touch, "after", [ANY] * len(arrays), VM, jax.ShapeDtypeStruct((8, BLOCK), F32), cost=cost
    )(*arrays)


def build_kernel(mixed, slots, tiles, _, *refs):
    weights, high, low, target_sum = (refs[i : i + USER_BLOCKS] for i in range(0, 4 * USER_BLOCKS, USER_BLOCKS))
    turn = lax.axis_index("dev") if mixed else 0
    for ref in weights + target_sum:
        ref[...] = jnp.zeros_like(ref)
    for tile in range(TILES_PER):
        for block in range(USER_BLOCKS):
            index = block * TILES_PER + tile
            first = (slots[0, index] ^ turn) * BLOCK
            columns = pl.ds(pl.multiple_of(first, BLOCK), BLOCK)
            confidence = tiles[index].astype(F32)
            target = jnp.where(confidence > 0, 1.0 + confidence, 0.0).astype(BF16)
            weights[block][:, columns] += confidence
            target_sum[block][:, columns] += target.astype(F32)
    for block in range(USER_BLOCKS):
        total = target_sum[block][...]
        top = total.astype(BF16)
        high[block][...] = top
        low[block][...] = (total - top.astype(F32)).astype(BF16)


def build_weights(slots, confidence, after, width, mixed):
    wide = jax.ShapeDtypeStruct((BLOCK, width), F32)
    narrow = jax.ShapeDtypeStruct((BLOCK, width), BF16)
    return call(
        functools.partial(build_kernel, mixed), "build_weights", [SM, VM, ANY],
        [VM] * 3 * USER_BLOCKS, [wide] * USER_BLOCKS + [narrow] * 2 * USER_BLOCKS,
        [pltpu.VMEM((BLOCK, width), F32)] * USER_BLOCKS, cost=None,
    )(slots, confidence, after)


def right_kernel(count, *refs):
    weights, high, low = (refs[i : i + USER_BLOCKS] for i in range(0, 3 * USER_BLOCKS, USER_BLOCKS))
    panels = refs[3 * USER_BLOCKS : 3 * USER_BLOCKS + count]
    items, items_t, right_side, image = refs[-4:]
    dot = functools.partial(jnp.dot, preferred_element_type=F32)
    for i in range(count):
        rows = slice(i * BLOCK, (i + 1) * BLOCK)
        panel = panels[i][0:BLOCK, :]
        items[rows, :] = panel
        items_t[:, rows] = panel.T
    for block in range(USER_BLOCKS):
        users = slice(block * BLOCK, (block + 1) * BLOCK)
        target = dot(high[block][...], items[...]) + dot(low[block][...], items[...])
        right_side[users, :] = target
        scores = dot(target.astype(BF16), items_t[...])
        image[users, :] = dot((weights[block][...] * scores).astype(BF16), items[...])


def start_solve(built, panels, after):
    width = built[0].shape[1]
    users = USER_BLOCKS * BLOCK
    return call(
        functools.partial(right_kernel, len(panels)), "right_side",
        [VM] * (len(built) + len(panels)) + [ANY], [VM] * 4,
        [shape(width), jax.ShapeDtypeStruct((RANK, width), BF16), shape(users, F32), shape(users, F32)],
        cost=None,
    )(*built, *panels, after)


def solve_kernel(halves, unroll, *refs):
    weights, refs = refs[:USER_BLOCKS], refs[USER_BLOCKS:]
    items, items_t, right_side, first_image = refs[:4]
    gram_parts, result, gram, sems = refs[4 : 4 + halves], refs[4 + halves], refs[5 + halves], refs[6 + halves]
    halves_ref, state = refs[7 + halves], refs[8 + halves :]
    residuals, directions, solved = (state[i : i + USER_BLOCKS] for i in range(0, 3 * USER_BLOCKS, USER_BLOCKS))
    dot = functools.partial(jnp.dot, preferred_element_type=F32)
    if halves == 1:
        gram[...] = gram_parts[0][...].astype(BF16)
    else:
        core = lax.rem(lax.axis_index("grp"), 2)
        for place, part in zip((core, 1 - core), gram_parts):
            halves_ref[place] = part[...].astype(F32)
        unpack_gram(halves_ref, gram)

    def rows(block):
        return slice(block * BLOCK, (block + 1) * BLOCK)

    def image_of(block, direction, scores):
        weighted = (weights[block][...] * scores).astype(BF16)
        return dot(weighted, items[...]) + dot(direction.astype(BF16), gram[...])

    def advance(block, norm_now, direction, residual, image, last=False):
        image = image + ridge * direction
        alpha = norm_now / jnp.sum(direction * image, axis=1, keepdims=True)
        solved[block][...] += alpha * direction
        if last:
            return norm_now
        residual = residual - alpha * image
        residuals[block][...] = residual
        norm_next = jnp.sum(residual * residual, axis=1, keepdims=True)
        directions[block][...] = residual + (norm_next / norm_now) * direction
        return norm_next

    norms = []
    for block in range(USER_BLOCKS):
        start = right_side[rows(block), :]
        solved[block][...] = jnp.zeros_like(start)
        norm = jnp.sum(start * start, axis=1, keepdims=True)
        image = first_image[rows(block), :] + dot(start.astype(BF16), gram[...])
        norms.append(advance(block, norm, start, start, image))

    copies = [
        pltpu.make_async_copy(solved[block], result.at[pl.ds(block * BLOCK, BLOCK), :], sems.at[block])
        for block in range(USER_BLOCKS)
    ]

    def step(_, norms, last=False):
        after = []
        for first in range(0, USER_BLOCKS, 2):
            pair = (first, first + 1)
            now = [directions[block][...] for block in pair]
            scores = [dot(direction.astype(BF16), items_t[...]) for direction in now]
            images = [image_of(*each) for each in zip(pair, now, scores)]
            for block, direction, image in zip(pair, now, images):
                after.append(advance(block, norms[block], direction, residuals[block][...], image, last))
                if last:
                    copies[block].start()
        return tuple(after)

    norms = lax.fori_loop(1, ITERS - 1, step, tuple(norms), unroll=unroll)
    step(None, norms, True)
    for copy in copies:
        copy.wait()


def solve_users(weights, started, gram_parts, unroll=True):
    users = USER_BLOCKS * BLOCK
    return call(
        functools.partial(solve_kernel, len(gram_parts), unroll), "solve_users",
        [VM] * (USER_BLOCKS + 4 + len(gram_parts)), ANY, shape(users, F32),
        [pltpu.VMEM((RANK, RANK), BF16), pltpu.SemaphoreType.DMA((USER_BLOCKS,)), pltpu.VMEM((2, PART, RANK), F32)]
        + [pltpu.VMEM((BLOCK, RANK), F32)] * 3 * USER_BLOCKS,
        cost=None,
    )(*weights, *started, *gram_parts)


def swap(array, group_bits, member_bits):
    order = [
        (g * 8 + d, (g ^ group_bits) * 8 + (d ^ member_bits)) for g in range(4) for d in range(8)
    ]
    return lax.ppermute(array, ("grp", "dev"), order)


def shards_4x8(item_factors, send_list, route_list, tile_slot, confidence):
    send_list, route_list = send_list.reshape(1, -1), route_list.reshape(1, -1)
    half, both = shape(BLOCK), shape(2 * BLOCK)
    part, total, near_shape = shape(PART), shape(PART, F32), shape(BLOCK + PART)
    out, panel_y, panel_own, gram, picks = call(
        first_kernel, "first", [VM] * 3 + [ANY], [VM] * 5,
        [shape(2 * BLOCK + PART), half, half, total, jax.ShapeDtypeStruct((8, BLOCK), jnp.int32)],
        [pltpu.VMEM((RANK, RANK), F32), pltpu.VMEM((2, PART, RANK), F32)],
    )(send_list, route_list, item_factors, after(LEAD))
    from_core = swap(out, 1, 0)
    out, gram_out, gram = call(pack_y, "pack_y", [VM] * 3, [VM] * 3, [both, part, total])(
        panel_y, gram, from_core
    )
    from_y = swap(out, 2, 0)
    gram_in = swap(gram_out, 0, 4)
    outs = call(
        pack_dev, "pack_dev", [VM] * 4, [VM] * 8, [half] * 8, [pltpu.VMEM((4, BLOCK, RANK), BF16)]
    )(picks, panel_own, from_core, from_y)
    panels = [outs[0]] + [None] * 7
    for k in (4, 6, 5, 7):
        panels[k] = swap(outs[k], 0, k)
    gram_out, gram = call(add_gram, "add_gram", [VM] * 2 + [ANY], [VM] * 2, [part, total])(
        gram, gram_in, after(COST // 4, gram_in)
    )
    gram_in = swap(gram_out, 2, 0)
    token = after(COST, panels[4])
    *near, gram = call(pack_near, "pack_near", [VM] * 5 + [ANY], [VM] * 4, [near_shape] * 3 + [total])(
        gram, gram_in, outs[1], outs[2], outs[3], token
    )
    for k in (3, 2, 1):
        panels[k] = swap(near[k - 1], 0, k)
    built = build_weights(tile_slot, confidence, after(0, panels[6], gram), 8 * BLOCK, True)
    token = after(COST, panels[5], panels[7])
    out, gram = call(last_gram, "last_gram", [VM] * 4 + [ANY] * 2, [VM] * 2, [part, total])(
        gram, panels[3], panels[2], panels[1], token, built[-1]
    )
    other = swap(out, 1, 0)
    started = start_solve(built, panels, gram)
    return solve_users(built[:USER_BLOCKS], started, [gram, other])


def shards(item_factors, send_list, route_list, tile_slot, confidence):
    partial_gram = lax.dot_general(
        item_factors, item_factors, (((0,), (0,)), ((), ())), preferred_element_type=F32
    )
    gram = lax.psum(partial_gram, ("grp", "dev"))
    own_panels = item_factors.reshape(PANELS_DEV, BLOCK, RANK)
    outgoing = own_panels[send_list[0].reshape(-1)]
    group_pool = lax.all_to_all(outgoing, "grp", split_axis=0, concat_axis=0, tiled=True)
    picked = group_pool[route_list[0].reshape(-1)]
    arrived = lax.all_to_all(picked, "dev", split_axis=0, concat_axis=0, tiled=True)
    count = arrived.shape[0]
    built = build_weights(tile_slot, confidence, gram, count * BLOCK, False)
    started = start_solve(built, [arrived[i] for i in range(count)], gram)
    return solve_users(built[:USER_BLOCKS], started, [gram], 1)


def solution(mesh):
    placed = (
        P(("grp", "dev"), None),
        P(("grp", "dev"), None, None),
        P(("grp", "dev"), None, None),
        P(("grp", "dev"), None),
        P(("grp", "dev"), None, None),
    )
    body = shards_4x8 if (mesh.shape["grp"], mesh.shape["dev"]) == (4, 8) else shards
    return jax.shard_map(
        body, mesh=mesh, in_specs=placed, out_specs=P(("grp", "dev"), None), check_vma=False
    )
```

```python
import functools

import jax
import jax.numpy as jnp
from jax import lax
from jax.experimental import pallas as pl
from jax.experimental.pallas import tpu as pltpu
from jax.sharding import PartitionSpec as P

RANK = 256
BLOCK = 128
PANELS_DEV = 2
USER_BLOCKS = 4
TILES_PER = 16
ITERS = 8
BF16 = jnp.bfloat16
F32 = jnp.float32

HALF = BLOCK // 2
PART = 3 * HALF // 2

ridge = 0.1
COST = 1000000000
LEAD = 3000000000

VM = pl.BlockSpec(memory_space=pltpu.VMEM)
ANY = pl.BlockSpec(memory_space=pl.ANY)
SM = pl.BlockSpec(memory_space=pltpu.SMEM)


def params():
    return pltpu.CompilerParams(vmem_limit_bytes=40 * 2**20)


def shape(rows, dtype=BF16):
    return jax.ShapeDtypeStruct((rows, RANK), dtype)


def call(body, name, in_specs, out_specs, out_shape, scratch=(), cost=0):
    return pl.pallas_call(
        body,
        in_specs=in_specs,
        out_specs=out_specs,
        out_shape=out_shape,
        scratch_shapes=list(scratch),
        compiler_params=params(),
        cost_estimate=None if cost is None else pl.CostEstimate(flops=cost, transcendentals=0, bytes_accessed=0),
        name=name,
    )


def own_panel(items, index):
    return items[pl.ds(pl.multiple_of(index * BLOCK, BLOCK), BLOCK), :]


def entry(row, index):
    place = lax.broadcasted_iota(jnp.int32, row.shape, 1)
    return jnp.max(jnp.where(place == index, row, 0))


def pack_gram(gram, parts):
    for core in range(2):
        rows = slice(core * BLOCK, (core + 1) * BLOCK)
        square = gram[rows, rows]
        side = gram[core * HALF : (core + 1) * HALF, BLOCK:]
        parts[core, 0:HALF, 0:BLOCK] = square[0:HALF, :]
        parts[core, 0:HALF, BLOCK:] = square[HALF:, :]
        parts[core, HALF:, 0:BLOCK] = side[0 : HALF // 2, :]
        parts[core, HALF:, BLOCK:] = side[HALF // 2 :, :]


def unpack_gram(parts, gram):
    for core in range(2):
        rows = slice(core * BLOCK, (core + 1) * BLOCK)
        half = slice(core * HALF, (core + 1) * HALF)
        part = parts[core]
        gram[rows, rows] = jnp.concatenate([part[0:HALF, 0:BLOCK], part[0:HALF, BLOCK:]], axis=0).astype(BF16)
        side = jnp.concatenate([part[HALF:, 0:BLOCK], part[HALF:, BLOCK:]], axis=0)
        gram[half, BLOCK:] = side.astype(BF16)
    gram[BLOCK:, 0:BLOCK] = gram[0:BLOCK, BLOCK:].T


def first_kernel(items, send, route, _, out, panel_y, panel_own, gram_own, picks, gram, parts):
    group = lax.axis_index("grp")
    member = lax.axis_index("dev")
    core = lax.rem(group, 2)
    panels, routes = send[...], route[...]
    out[0:BLOCK, :] = own_panel(items, entry(panels, group ^ 1))
    out[BLOCK : 2 * BLOCK, :] = own_panel(items, entry(panels, group ^ 3))
    panel_y[...] = own_panel(items, entry(panels, group ^ 2))
    panel_own[...] = own_panel(items, entry(panels, group))
    rows = items[...]
    gram[...] = lax.dot_general(rows, rows, (((0,), (0,)), ((), ())), preferred_element_type=F32)
    pack_gram(gram, parts)
    out[2 * BLOCK :, :] = parts[1 - core].astype(BF16)
    gram_own[...] = parts[core]
    for step in range(8):
        picks[step : step + 1, :] = jnp.full((1, BLOCK), entry(routes, member ^ step) ^ group, jnp.int32)


def pack_y(panel_y, gram_own, from_core, out, gram_out, gram_sum):
    out[0:BLOCK, :] = panel_y[...]
    out[BLOCK : 2 * BLOCK, :] = from_core[BLOCK : 2 * BLOCK, :]
    total = gram_own[...] + from_core[2 * BLOCK :, :].astype(F32)
    gram_out[...] = total.astype(BF16)
    gram_sum[...] = total


def pack_dev(picks, panel_own, from_core, from_y, *refs):
    outs, pool = refs[:8], refs[8]
    pool[0] = panel_own[...]
    pool[1] = from_core[0:BLOCK, :]
    pool[2] = from_y[0:BLOCK, :]
    pool[3] = from_y[BLOCK : 2 * BLOCK, :]
    for step in range(8):
        outs[step][...] = pool[jnp.max(picks[step : step + 1, :])]


def add_gram(gram_own, arrived, _, out, gram_sum):
    total = gram_own[...] + arrived[...].astype(F32)
    out[...] = total.astype(BF16)
    gram_sum[...] = total


def pack_near(gram_own, arrived, *refs):
    panels, outs, gram_sum = refs[:3], refs[4:7], refs[7]
    total = gram_own[...] + arrived[...].astype(F32)
    gram_sum[...] = total
    for panel, out in zip(panels, outs):
        out[0:BLOCK, :] = panel[...]
        out[BLOCK:, :] = total.astype(BF16)


def last_gram(gram_own, *refs):
    out, gram_sum = refs[-2:]
    total = gram_own[...]
    for part in refs[:3]:
        total += part[BLOCK:, :].astype(F32)
    out[...] = total.astype(BF16)
    gram_sum[...] = total


def touch(*refs):
    refs[-1][...] = jnp.zeros_like(refs[-1])


def after(cost, *arrays):
    return call(
        touch, "after", [ANY] * len(arrays), VM, jax.ShapeDtypeStruct((8, BLOCK), F32), cost=cost
    )(*arrays)


def build_kernel(mixed, slots, tiles, _, *refs):
    weights, high, low, target_sum = (refs[i : i + USER_BLOCKS] for i in range(0, 4 * USER_BLOCKS, USER_BLOCKS))
    turn = lax.axis_index("dev") if mixed else 0
    for ref in weights + target_sum:
        ref[...] = jnp.zeros_like(ref)
    for tile in range(TILES_PER):
        for block in range(USER_BLOCKS):
            index = block * TILES_PER + tile
            first = (slots[0, index] ^ turn) * BLOCK
            columns = pl.ds(pl.multiple_of(first, BLOCK), BLOCK)
            confidence = tiles[index].astype(F32)
            target = jnp.where(confidence > 0, 1.0 + confidence, 0.0).astype(BF16)
            weights[block][:, columns] += confidence
            target_sum[block][:, columns] += target.astype(F32)
    for block in range(USER_BLOCKS):
        total = target_sum[block][...]
        top = total.astype(BF16)
        high[block][...] = top
        low[block][...] = (total - top.astype(F32)).astype(BF16)


def build_weights(slots, confidence, after, width, mixed):
    wide = jax.ShapeDtypeStruct((BLOCK, width), F32)
    narrow = jax.ShapeDtypeStruct((BLOCK, width), BF16)
    return call(
        functools.partial(build_kernel, mixed), "build_weights", [SM, VM, ANY],
        [VM] * 3 * USER_BLOCKS, [wide] * USER_BLOCKS + [narrow] * 2 * USER_BLOCKS,
        [pltpu.VMEM((BLOCK, width), F32)] * USER_BLOCKS, cost=None,
    )(slots, confidence, after)


def right_kernel(count, *refs):
    weights, high, low = (refs[i : i + USER_BLOCKS] for i in range(0, 3 * USER_BLOCKS, USER_BLOCKS))
    panels = refs[3 * USER_BLOCKS : 3 * USER_BLOCKS + count]
    items, items_t, right_side, image = refs[-4:]
    dot = functools.partial(jnp.dot, preferred_element_type=F32)
    for i in range(count):
        rows = slice(i * BLOCK, (i + 1) * BLOCK)
        panel = panels[i][0:BLOCK, :]
        items[rows, :] = panel
        items_t[:, rows] = panel.T
    targets = [dot(high[block][...], items[...]) + dot(low[block][...], items[...]) for block in range(USER_BLOCKS)]
    for first in range(0, USER_BLOCKS, 2):
        pair = (first, first + 1)
        scores = [dot(targets[block].astype(BF16), items_t[...]) for block in pair]
        for block, score in zip(pair, scores):
            users = slice(block * BLOCK, (block + 1) * BLOCK)
            right_side[users, :] = targets[block]
            image[users, :] = dot((weights[block][...] * score).astype(BF16), items[...])


def start_solve(built, panels, after):
    width = built[0].shape[1]
    users = USER_BLOCKS * BLOCK
    return call(
        functools.partial(right_kernel, len(panels)), "right_side",
        [VM] * (len(built) + len(panels)) + [ANY], [VM] * 4,
        [shape(width), jax.ShapeDtypeStruct((RANK, width), BF16), shape(users, F32), shape(users, F32)],
        cost=None,
    )(*built, *panels, after)


def solve_kernel(halves, unroll, *refs):
    weights, refs = refs[:USER_BLOCKS], refs[USER_BLOCKS:]
    items, items_t, right_side, first_image = refs[:4]
    gram_parts, result, gram, sems = refs[4 : 4 + halves], refs[4 + halves], refs[5 + halves], refs[6 + halves]
    halves_ref, state = refs[7 + halves], refs[8 + halves :]
    residuals, directions, solved = (state[i : i + USER_BLOCKS] for i in range(0, 3 * USER_BLOCKS, USER_BLOCKS))
    dot = functools.partial(jnp.dot, preferred_element_type=F32)
    if halves == 1:
        gram[...] = gram_parts[0][...].astype(BF16)
    else:
        core = lax.rem(lax.axis_index("grp"), 2)
        for place, part in zip((core, 1 - core), gram_parts):
            halves_ref[place] = part[...].astype(F32)
        unpack_gram(halves_ref, gram)

    def rows(block):
        return slice(block * BLOCK, (block + 1) * BLOCK)

    def image_of(block, direction, scores):
        weighted = (weights[block][...] * scores).astype(BF16)
        return dot(weighted, items[...]) + dot(direction.astype(BF16), gram[...])

    def advance(block, norm_now, direction, residual, image, last=False):
        image = image + ridge * direction
        alpha = norm_now / jnp.sum(direction * image, axis=1, keepdims=True)
        solved[block][...] += alpha * direction
        if last:
            return norm_now
        residual = residual - alpha * image
        residuals[block][...] = residual
        norm_next = jnp.sum(residual * residual, axis=1, keepdims=True)
        directions[block][...] = residual + (norm_next / norm_now) * direction
        return norm_next

    norms = []
    for block in range(USER_BLOCKS):
        start = right_side[rows(block), :]
        solved[block][...] = jnp.zeros_like(start)
        norm = jnp.sum(start * start, axis=1, keepdims=True)
        image = first_image[rows(block), :] + dot(start.astype(BF16), gram[...])
        norms.append(advance(block, norm, start, start, image))

    copies = [
        pltpu.make_async_copy(solved[block], result.at[pl.ds(block * BLOCK, BLOCK), :], sems.at[block])
        for block in range(USER_BLOCKS)
    ]

    def step(_, norms, last=False):
        after = []
        for first in range(0, USER_BLOCKS, 2):
            pair = (first, first + 1)
            now = [directions[block][...] for block in pair]
            scores = [dot(direction.astype(BF16), items_t[...]) for direction in now]
            images = [image_of(*each) for each in zip(pair, now, scores)]
            for block, direction, image in zip(pair, now, images):
                after.append(advance(block, norms[block], direction, residuals[block][...], image, last))
                if last:
                    copies[block].start()
        return tuple(after)

    norms = lax.fori_loop(1, ITERS - 1, step, tuple(norms), unroll=unroll)
    step(None, norms, True)
    for copy in copies:
        copy.wait()


def solve_users(weights, started, gram_parts, unroll=True):
    users = USER_BLOCKS * BLOCK
    return call(
        functools.partial(solve_kernel, len(gram_parts), unroll), "solve_users",
        [VM] * (USER_BLOCKS + 4 + len(gram_parts)), ANY, shape(users, F32),
        [pltpu.VMEM((RANK, RANK), BF16), pltpu.SemaphoreType.DMA((USER_BLOCKS,)), pltpu.VMEM((2, PART, RANK), F32)]
        + [pltpu.VMEM((BLOCK, RANK), F32)] * 3 * USER_BLOCKS,
        cost=None,
    )(*weights, *started, *gram_parts)


def swap(array, group_bits, member_bits):
    order = [
        (g * 8 + d, (g ^ group_bits) * 8 + (d ^ member_bits)) for g in range(4) for d in range(8)
    ]
    return lax.ppermute(array, ("grp", "dev"), order)


def shards_4x8(item_factors, send_list, route_list, tile_slot, confidence):
    send_list, route_list = send_list.reshape(1, -1), route_list.reshape(1, -1)
    half, both = shape(BLOCK), shape(2 * BLOCK)
    part, total, near_shape = shape(PART), shape(PART, F32), shape(BLOCK + PART)
    out, panel_y, panel_own, gram, picks = call(
        first_kernel, "first", [VM] * 3 + [ANY], [VM] * 5,
        [shape(2 * BLOCK + PART), half, half, total, jax.ShapeDtypeStruct((8, BLOCK), jnp.int32)],
        [pltpu.VMEM((RANK, RANK), F32), pltpu.VMEM((2, PART, RANK), F32)],
    )(item_factors, send_list, route_list, after(LEAD))
    from_core = swap(out, 1, 0)
    out, gram_out, gram = call(pack_y, "pack_y", [VM] * 3, [VM] * 3, [both, part, total])(
        panel_y, gram, from_core
    )
    from_y = swap(out, 2, 0)
    gram_in = swap(gram_out, 0, 4)
    outs = call(
        pack_dev, "pack_dev", [VM] * 4, [VM] * 8, [half] * 8, [pltpu.VMEM((4, BLOCK, RANK), BF16)]
    )(picks, panel_own, from_core, from_y)
    panels = [outs[0]] + [None] * 7
    for k in (4, 7, 5, 6):
        panels[k] = swap(outs[k], 0, k)
    gram_out, gram = call(add_gram, "add_gram", [VM] * 2 + [ANY], [VM] * 2, [part, total])(
        gram, gram_in, after(COST // 4, gram_in)
    )
    gram_in = swap(gram_out, 2, 0)
    token = after(COST, panels[4])
    *near, gram = call(pack_near, "pack_near", [VM] * 5 + [ANY], [VM] * 4, [near_shape] * 3 + [total])(
        gram, gram_in, outs[1], outs[2], outs[3], token
    )
    for k in (3, 2, 1):
        panels[k] = swap(near[k - 1], 0, k)
    built = build_weights(tile_slot, confidence, after(0, panels[7], gram), 8 * BLOCK, True)
    token = after(COST, panels[5], panels[6])
    out, gram = call(last_gram, "last_gram", [VM] * 4 + [ANY] * 2, [VM] * 2, [part, total])(
        gram, panels[3], panels[2], panels[1], token, built[-1]
    )
    other = swap(out, 1, 0)
    started = start_solve(built, panels, gram)
    return solve_users(built[:USER_BLOCKS], started, [gram, other])


def shards(item_factors, send_list, route_list, tile_slot, confidence):
    partial_gram = lax.dot_general(
        item_factors, item_factors, (((0,), (0,)), ((), ())), preferred_element_type=F32
    )
    gram = lax.psum(partial_gram, ("grp", "dev"))
    own_panels = item_factors.reshape(PANELS_DEV, BLOCK, RANK)
    outgoing = own_panels[send_list[0].reshape(-1)]
    group_pool = lax.all_to_all(outgoing, "grp", split_axis=0, concat_axis=0, tiled=True)
    picked = group_pool[route_list[0].reshape(-1)]
    arrived = lax.all_to_all(picked, "dev", split_axis=0, concat_axis=0, tiled=True)
    count = arrived.shape[0]
    built = build_weights(tile_slot, confidence, gram, count * BLOCK, False)
    started = start_solve(built, [arrived[i] for i in range(count)], gram)
    return solve_users(built[:USER_BLOCKS], started, [gram], 1)


def solution(mesh):
    placed = (
        P(("grp", "dev"), None),
        P(("grp", "dev"), None, None),
        P(("grp", "dev"), None, None),
        P(("grp", "dev"), None),
        P(("grp", "dev"), None, None),
    )
    body = shards_4x8 if (mesh.shape["grp"], mesh.shape["dev"]) == (4, 8) else shards
    return jax.shard_map(
        body, mesh=mesh, in_specs=placed, out_specs=P(("grp", "dev"), None), check_vma=False
    )
```

```python
import functools

import jax
import jax.numpy as jnp
from jax import lax
from jax.experimental import pallas as pl
from jax.experimental.pallas import tpu as pltpu
from jax.sharding import PartitionSpec as P

RANK = 256
BLOCK = 128
PANELS_DEV = 2
USER_BLOCKS = 4
TILES_PER = 16
ITERS = 8
BF16 = jnp.bfloat16
F32 = jnp.float32

HALF = BLOCK // 2
PART = 3 * HALF // 2

ridge = 0.1
COST = 1000000000
LEAD = 3000000000

VM = pl.BlockSpec(memory_space=pltpu.VMEM)
ANY = pl.BlockSpec(memory_space=pl.ANY)
SM = pl.BlockSpec(memory_space=pltpu.SMEM)


def params():
    return pltpu.CompilerParams(vmem_limit_bytes=40 * 2**20)


def shape(rows, dtype=BF16):
    return jax.ShapeDtypeStruct((rows, RANK), dtype)


def call(body, name, in_specs, out_specs, out_shape, scratch=(), cost=0):
    return pl.pallas_call(
        body,
        in_specs=in_specs,
        out_specs=out_specs,
        out_shape=out_shape,
        scratch_shapes=list(scratch),
        compiler_params=params(),
        cost_estimate=None if cost is None else pl.CostEstimate(flops=cost, transcendentals=0, bytes_accessed=0),
        name=name,
    )


def own_panel(items, index):
    return items[pl.ds(pl.multiple_of(index * BLOCK, BLOCK), BLOCK), :]


def entry(row, index):
    place = lax.broadcasted_iota(jnp.int32, row.shape, 1)
    return jnp.max(jnp.where(place == index, row, 0))


def pack_gram(gram, parts):
    for core in range(2):
        rows = slice(core * BLOCK, (core + 1) * BLOCK)
        square = gram[rows, rows]
        side = gram[core * HALF : (core + 1) * HALF, BLOCK:]
        parts[core, 0:HALF, 0:BLOCK] = square[0:HALF, :]
        parts[core, 0:HALF, BLOCK:] = square[HALF:, :]
        parts[core, HALF:, 0:BLOCK] = side[0 : HALF // 2, :]
        parts[core, HALF:, BLOCK:] = side[HALF // 2 :, :]


def unpack_gram(parts, gram):
    for core in range(2):
        rows = slice(core * BLOCK, (core + 1) * BLOCK)
        half = slice(core * HALF, (core + 1) * HALF)
        part = parts[core]
        gram[rows, rows] = jnp.concatenate([part[0:HALF, 0:BLOCK], part[0:HALF, BLOCK:]], axis=0).astype(BF16)
        side = jnp.concatenate([part[HALF:, 0:BLOCK], part[HALF:, BLOCK:]], axis=0)
        gram[half, BLOCK:] = side.astype(BF16)
    gram[BLOCK:, 0:BLOCK] = gram[0:BLOCK, BLOCK:].T


def first_kernel(items, send, route, _, out, panel_y, panel_own, gram_own, picks, gram, parts):
    group = lax.axis_index("grp")
    member = lax.axis_index("dev")
    core = lax.rem(group, 2)
    panels, routes = send[...], route[...]
    out[0:BLOCK, :] = own_panel(items, entry(panels, group ^ 1))
    out[BLOCK : 2 * BLOCK, :] = own_panel(items, entry(panels, group ^ 3))
    panel_y[...] = own_panel(items, entry(panels, group ^ 2))
    panel_own[...] = own_panel(items, entry(panels, group))
    rows = items[...]
    gram[...] = lax.dot_general(rows, rows, (((0,), (0,)), ((), ())), preferred_element_type=F32)
    pack_gram(gram, parts)
    out[2 * BLOCK :, :] = parts[1 - core].astype(BF16)
    gram_own[...] = parts[core]
    for step in range(8):
        picks[step : step + 1, :] = jnp.full((1, BLOCK), entry(routes, member ^ step) ^ group, jnp.int32)


def pack_y(panel_y, gram_own, from_core, out, gram_out, gram_sum):
    out[0:BLOCK, :] = panel_y[...]
    out[BLOCK : 2 * BLOCK, :] = from_core[BLOCK : 2 * BLOCK, :]
    total = gram_own[...] + from_core[2 * BLOCK :, :].astype(F32)
    gram_out[...] = total.astype(BF16)
    gram_sum[...] = total


def pack_dev(picks, panel_own, from_core, from_y, *refs):
    outs, pool = refs[:8], refs[8]
    pool[0] = panel_own[...]
    pool[1] = from_core[0:BLOCK, :]
    pool[2] = from_y[0:BLOCK, :]
    pool[3] = from_y[BLOCK : 2 * BLOCK, :]
    for step in range(8):
        outs[step][...] = pool[jnp.max(picks[step : step + 1, :])]


def add_gram(gram_own, arrived, _, out, gram_sum):
    total = gram_own[...] + arrived[...].astype(F32)
    out[...] = total.astype(BF16)
    gram_sum[...] = total


def pack_near(gram_own, arrived, *refs):
    panels, outs, gram_sum = refs[:3], refs[4:7], refs[7]
    total = gram_own[...] + arrived[...].astype(F32)
    gram_sum[...] = total
    for panel, out in zip(panels, outs):
        out[0:BLOCK, :] = panel[...]
        out[BLOCK:, :] = total.astype(BF16)


def last_gram(gram_own, *refs):
    out, gram_sum = refs[-2:]
    total = gram_own[...]
    for part in refs[:3]:
        total += part[BLOCK:, :].astype(F32)
    out[...] = total.astype(BF16)
    gram_sum[...] = total


def touch(*refs):
    refs[-1][...] = jnp.zeros_like(refs[-1])


def after(cost, *arrays):
    return call(
        touch, "after", [ANY] * len(arrays), VM, jax.ShapeDtypeStruct((8, BLOCK), F32), cost=cost
    )(*arrays)


def build_kernel(mixed, slots, tiles, _, *refs):
    weights, high, low, target_sum = (refs[i : i + USER_BLOCKS] for i in range(0, 4 * USER_BLOCKS, USER_BLOCKS))
    turn = lax.axis_index("dev") if mixed else 0
    for ref in weights + target_sum:
        ref[...] = jnp.zeros_like(ref)
    for tile in range(TILES_PER):
        for block in range(USER_BLOCKS):
            index = block * TILES_PER + tile
            first = (slots[0, index] ^ turn) * BLOCK
            columns = pl.ds(pl.multiple_of(first, BLOCK), BLOCK)
            confidence = tiles[index].astype(F32)
            target = jnp.where(confidence > 0, 1.0 + confidence, 0.0).astype(BF16)
            weights[block][:, columns] += confidence
            target_sum[block][:, columns] += target.astype(F32)
    for block in range(USER_BLOCKS):
        total = target_sum[block][...]
        top = total.astype(BF16)
        high[block][...] = top
        low[block][...] = (total - top.astype(F32)).astype(BF16)


def build_weights(slots, confidence, after, width, mixed):
    wide = jax.ShapeDtypeStruct((BLOCK, width), F32)
    narrow = jax.ShapeDtypeStruct((BLOCK, width), BF16)
    return call(
        functools.partial(build_kernel, mixed), "build_weights", [SM, VM, ANY],
        [VM] * 3 * USER_BLOCKS, [wide] * USER_BLOCKS + [narrow] * 2 * USER_BLOCKS,
        [pltpu.VMEM((BLOCK, width), F32)] * USER_BLOCKS, cost=None,
    )(slots, confidence, after)


def right_kernel(count, *refs):
    weights, high, low = (refs[i : i + USER_BLOCKS] for i in range(0, 3 * USER_BLOCKS, USER_BLOCKS))
    panels = refs[3 * USER_BLOCKS : 3 * USER_BLOCKS + count]
    items, items_t, right_side, image = refs[-4:]
    dot = functools.partial(jnp.dot, preferred_element_type=F32)
    for i in range(count):
        rows = slice(i * BLOCK, (i + 1) * BLOCK)
        panel = panels[i][0:BLOCK, :]
        items[rows, :] = panel
        items_t[:, rows] = panel.T
    targets = [dot(high[block][...], items[...]) + dot(low[block][...], items[...]) for block in range(USER_BLOCKS)]
    scores = [dot(target.astype(BF16), items_t[...]) for target in targets]
    for block, (target, score) in enumerate(zip(targets, scores)):
        users = slice(block * BLOCK, (block + 1) * BLOCK)
        right_side[users, :] = target
        image[users, :] = dot((weights[block][...] * score).astype(BF16), items[...])


def start_solve(built, panels, after):
    width = built[0].shape[1]
    users = USER_BLOCKS * BLOCK
    return call(
        functools.partial(right_kernel, len(panels)), "right_side",
        [VM] * (len(built) + len(panels)) + [ANY], [VM] * 4,
        [shape(width), jax.ShapeDtypeStruct((RANK, width), BF16), shape(users, F32), shape(users, F32)],
        cost=None,
    )(*built, *panels, after)


def solve_kernel(halves, unroll, *refs):
    weights, refs = refs[:USER_BLOCKS], refs[USER_BLOCKS:]
    items, items_t, right_side, first_image = refs[:4]
    gram_parts, result, gram, sems = refs[4 : 4 + halves], refs[4 + halves], refs[5 + halves], refs[6 + halves]
    halves_ref, state = refs[7 + halves], refs[8 + halves :]
    residuals, directions, solved = (state[i : i + USER_BLOCKS] for i in range(0, 3 * USER_BLOCKS, USER_BLOCKS))
    dot = functools.partial(jnp.dot, preferred_element_type=F32)
    if halves == 1:
        gram[...] = gram_parts[0][...].astype(BF16)
    else:
        core = lax.rem(lax.axis_index("grp"), 2)
        for place, part in zip((core, 1 - core), gram_parts):
            halves_ref[place] = part[...].astype(F32)
        unpack_gram(halves_ref, gram)

    def rows(block):
        return slice(block * BLOCK, (block + 1) * BLOCK)

    def image_of(block, direction, scores):
        weighted = (weights[block][...] * scores).astype(BF16)
        return dot(weighted, items[...]) + dot(direction.astype(BF16), gram[...])

    def advance(block, norm_now, direction, residual, image, last=False):
        image = image + ridge * direction
        alpha = norm_now / jnp.sum(direction * image, axis=1, keepdims=True)
        solved[block][...] += alpha * direction
        if last:
            return norm_now
        residual = residual - alpha * image
        residuals[block][...] = residual
        norm_next = jnp.sum(residual * residual, axis=1, keepdims=True)
        directions[block][...] = residual + (norm_next / norm_now) * direction
        return norm_next

    norms = []
    for block in range(USER_BLOCKS):
        start = right_side[rows(block), :]
        solved[block][...] = jnp.zeros_like(start)
        norm = jnp.sum(start * start, axis=1, keepdims=True)
        image = first_image[rows(block), :] + dot(start.astype(BF16), gram[...])
        norms.append(advance(block, norm, start, start, image))

    copies = [
        pltpu.make_async_copy(solved[block], result.at[pl.ds(block * BLOCK, BLOCK), :], sems.at[block])
        for block in range(USER_BLOCKS)
    ]

    def step(_, norms, last=False):
        after = []
        for first in range(0, USER_BLOCKS, 2):
            pair = (first, first + 1)
            now = [directions[block][...] for block in pair]
            scores = [dot(direction.astype(BF16), items_t[...]) for direction in now]
            images = [image_of(*each) for each in zip(pair, now, scores)]
            for block, direction, image in zip(pair, now, images):
                after.append(advance(block, norms[block], direction, residuals[block][...], image, last))
                if last:
                    copies[block].start()
        return tuple(after)

    norms = lax.fori_loop(1, ITERS - 1, step, tuple(norms), unroll=unroll)
    step(None, norms, True)
    for copy in copies:
        copy.wait()


def solve_users(weights, started, gram_parts, unroll=True):
    users = USER_BLOCKS * BLOCK
    return call(
        functools.partial(solve_kernel, len(gram_parts), unroll), "solve_users",
        [VM] * (USER_BLOCKS + 4 + len(gram_parts)), ANY, shape(users, F32),
        [pltpu.VMEM((RANK, RANK), BF16), pltpu.SemaphoreType.DMA((USER_BLOCKS,)), pltpu.VMEM((2, PART, RANK), F32)]
        + [pltpu.VMEM((BLOCK, RANK), F32)] * 3 * USER_BLOCKS,
        cost=None,
    )(*weights, *started, *gram_parts)


def swap(array, group_bits, member_bits):
    order = [
        (g * 8 + d, (g ^ group_bits) * 8 + (d ^ member_bits)) for g in range(4) for d in range(8)
    ]
    return lax.ppermute(array, ("grp", "dev"), order)


def shards_4x8(item_factors, send_list, route_list, tile_slot, confidence):
    send_list, route_list = send_list.reshape(1, -1), route_list.reshape(1, -1)
    half, both = shape(BLOCK), shape(2 * BLOCK)
    part, total, near_shape = shape(PART), shape(PART, F32), shape(BLOCK + PART)
    out, panel_y, panel_own, gram, picks = call(
        first_kernel, "first", [VM] * 3 + [ANY], [VM] * 5,
        [shape(2 * BLOCK + PART), half, half, total, jax.ShapeDtypeStruct((8, BLOCK), jnp.int32)],
        [pltpu.VMEM((RANK, RANK), F32), pltpu.VMEM((2, PART, RANK), F32)],
    )(item_factors, send_list, route_list, after(LEAD))
    from_core = swap(out, 1, 0)
    out, gram_out, gram = call(pack_y, "pack_y", [VM] * 3, [VM] * 3, [both, part, total])(
        panel_y, gram, from_core
    )
    from_y = swap(out, 2, 0)
    gram_in = swap(gram_out, 0, 4)
    outs = call(
        pack_dev, "pack_dev", [VM] * 4, [VM] * 8, [half] * 8, [pltpu.VMEM((4, BLOCK, RANK), BF16)]
    )(picks, panel_own, from_core, from_y)
    panels = [outs[0]] + [None] * 7
    for k in (4, 7, 5, 6):
        panels[k] = swap(outs[k], 0, k)
    gram_out, gram = call(add_gram, "add_gram", [VM] * 2 + [ANY], [VM] * 2, [part, total])(
        gram, gram_in, after(COST // 4, gram_in)
    )
    gram_in = swap(gram_out, 2, 0)
    token = after(COST, panels[4])
    *near, gram = call(pack_near, "pack_near", [VM] * 5 + [ANY], [VM] * 4, [near_shape] * 3 + [total])(
        gram, gram_in, outs[1], outs[2], outs[3], token
    )
    for k in (3, 2, 1):
        panels[k] = swap(near[k - 1], 0, k)
    built = build_weights(tile_slot, confidence, after(0, panels[7], gram), 8 * BLOCK, True)
    token = after(COST, panels[5], panels[6])
    out, gram = call(last_gram, "last_gram", [VM] * 4 + [ANY] * 2, [VM] * 2, [part, total])(
        gram, panels[3], panels[2], panels[1], token, built[-1]
    )
    other = swap(out, 1, 0)
    started = start_solve(built, panels, gram)
    return solve_users(built[:USER_BLOCKS], started, [gram, other])


def shards(item_factors, send_list, route_list, tile_slot, confidence):
    partial_gram = lax.dot_general(
        item_factors, item_factors, (((0,), (0,)), ((), ())), preferred_element_type=F32
    )
    gram = lax.psum(partial_gram, ("grp", "dev"))
    own_panels = item_factors.reshape(PANELS_DEV, BLOCK, RANK)
    outgoing = own_panels[send_list[0].reshape(-1)]
    group_pool = lax.all_to_all(outgoing, "grp", split_axis=0, concat_axis=0, tiled=True)
    picked = group_pool[route_list[0].reshape(-1)]
    arrived = lax.all_to_all(picked, "dev", split_axis=0, concat_axis=0, tiled=True)
    count = arrived.shape[0]
    built = build_weights(tile_slot, confidence, gram, count * BLOCK, False)
    started = start_solve(built, [arrived[i] for i in range(count)], gram)
    return solve_users(built[:USER_BLOCKS], started, [gram], 1)


def solution(mesh):
    placed = (
        P(("grp", "dev"), None),
        P(("grp", "dev"), None, None),
        P(("grp", "dev"), None, None),
        P(("grp", "dev"), None),
        P(("grp", "dev"), None, None),
    )
    body = shards_4x8 if (mesh.shape["grp"], mesh.shape["dev"]) == (4, 8) else shards
    return jax.shard_map(
        body, mesh=mesh, in_specs=placed, out_specs=P(("grp", "dev"), None), check_vma=False
    )
```
